32 devices in a mesh: blk: 8 (over z, x), dp: 4 (over y, core).
Axes of the slice: x: 2, y: 2, z: 4, core: 2. Of those that a mesh axis runs over, the one named last changes fastest.
Arguments:
- audio_frames: bfloat16 [4, 512, 16, 1024], P('dp', 'blk'), may hold values from -6 to 6
- conv_weight: bfloat16 [3072, 1024], replicated, may hold values from -0.109375 to 0.109375
- proj_weight: bfloat16 [1024, 512], replicated, may hold values from -0.1875 to 0.1875
- text_embed: bfloat16 [4, 512, 512], P('dp', 'blk'), may hold values from -6 to 6
- pair_langs: int32 [4, 512], P('dp', 'blk'), may hold values from 0 to 99, as said below
- log_scale: float32 [100], replicated, may hold values from 2 to 5
- lang_bias: float32 [100], replicated, may hold values from 95 to 105
- log_var: float32 [100], replicated, may hold values from -1 to 1
Outputs:
- loss: float32 [], replicated
- scale_grad: float32 [100], replicated
- var_grad: float32 [100], replicated
- conv_grad: float32 [3072, 1024], P('blk', 'dp')
- proj_grad: float32 [1024, 512], P('blk', 'dp')
- text_grad: float32 [4, 512, 512], P('dp', 'blk')
The draws below stay inside these ranges and needn't reach their ends.
Inputs may be any that keep to these rules, and one draw needn't show every extreme that they name: `pair_langs`: language ids of the pairs; in every draw some languages are named by no pair.
All inputs are finite; a program needn't handle non-finite values.
Results may differ from the reference program's by a relative error of at most 0.029.
Values may be sent and summed in bfloat16 or wider, within the bound.
A program may use at most 128 MiB of HBM per device.

```python
import jax
import jax.numpy as jnp
from jax import lax

CIN = 1024
WIDTH = 1024
EMB = 512
LANGS = 100
FRAMES = 16
GROUP = 512
N_DP = 4


def draw_pair_langs(key, part):
    order_key, first_key, second_key = jax.random.split(jax.random.fold_in(key, 17), 3)
    language_order = jax.random.permutation(order_key, LANGS).astype(jnp.int32)
    first_pick = jax.random.randint(first_key, (N_DP, GROUP), 0, LANGS - 3, dtype=jnp.int32)
    second_pick = jax.random.randint(second_key, (N_DP, GROUP), 0, LANGS - 3, dtype=jnp.int32)
    rank_index = jnp.minimum(first_pick, second_pick) + 3
    return jnp.take(language_order, rank_index).astype(jnp.int32)


def level_of(stream_key, extent, cuts, least, high):
    def one(axis_at, parts):
        heights = jax.random.uniform(jax.random.fold_in(jax.random.fold_in(stream_key, 6), axis_at), (parts,), jnp.float32, least / len(cuts), high / len(cuts))
        return jnp.repeat(jnp.exp(heights), extent[axis_at] // parts).reshape((-1,) + (1,) * (len(extent) - axis_at - 1))

    factor_of = one(*cuts[0])
    for cut in cuts[1:]:
        factor_of = factor_of * one(*cut)
    return factor_of


def centred(key, extent, scale, reach, pieces=(), held_as=jnp.bfloat16):
    drawn = jax.random.normal(key, extent, jnp.float32) * scale
    if len(pieces) > 0:
        drawn = level_of(key, extent, pieces, -0.22, 0.18) * drawn
    return jnp.clip(drawn, min=-reach, max=reach).astype(held_as)


def setup_inputs(seed: int = 0) -> dict:
    key_list = jax.random.split(jax.random.key(seed), 9)
    audio_frames = centred(key_list[0], (N_DP, GROUP, FRAMES, CIN), 1.0, 6.0, ((0, 4), (1, 8)))
    conv_weight = centred(key_list[1], (3 * CIN, WIDTH), (3 * CIN) ** -0.5, 0.109375)
    proj_weight = centred(key_list[2], (WIDTH, EMB), WIDTH ** -0.5, 0.1875)
    text_embed = centred(key_list[3], (N_DP, GROUP, EMB), 1.0, 6.0, ((0, 4), (1, 8)))
    pair_langs = draw_pair_langs(jax.random.fold_in(key_list[8], 71), 0)
    log_scale = jnp.clip(jax.random.uniform(key_list[5], (LANGS,), jnp.float32, 2.0, 5.0), 2.0, 5.0)
    lang_bias = jnp.clip(jax.random.uniform(key_list[6], (LANGS,), jnp.float32, 95.0, 105.0), 95.0, 105.0)
    log_var = jnp.clip(jax.random.uniform(key_list[7], (LANGS,), jnp.float32, -1.0, 1.0), -1.0, 1.0)
    return dict(audio_frames=audio_frames, conv_weight=conv_weight, proj_weight=proj_weight, text_embed=text_embed, pair_langs=pair_langs, log_scale=log_scale, lang_bias=lang_bias, log_var=log_var)


epsilon = 1e-06

def stack_taps(frames):
    clips, steps_count, channels = frames.shape
    blank = jnp.zeros_like(frames[:, :1])
    before = jnp.concatenate([blank, frames[:, :-1]], axis=1)
    after = jnp.concatenate([frames[:, 1:], blank], axis=1)
    return jnp.concatenate([before, frames, after], axis=2).reshape(clips * steps_count, 3 * channels)

def encode(frames, conv_weight, proj_weight):
    clips, steps_count, channels = frames.shape
    stacked = stack_taps(frames)
    preact = jnp.dot(stacked, conv_weight, preferred_element_type=jnp.float32)
    pooled = lax.optimization_barrier(jnp.mean(jax.nn.gelu(preact).reshape(clips, steps_count, -1), axis=1)).astype(jnp.bfloat16)
    embedding = jnp.dot(pooled, proj_weight, preferred_element_type=jnp.float32)
    audio_len = jnp.sqrt(lax.optimization_barrier(jnp.sum(embedding * embedding, axis=-1, keepdims=True)) + epsilon)
    return (stacked, preact, pooled, embedding / audio_len, audio_len)

def normalize_text(text_rows):
    text_float = text_rows.astype(jnp.float32)
    text_len = jnp.sqrt(lax.optimization_barrier(jnp.sum(text_float * text_float, axis=-1, keepdims=True)) + epsilon)
    return (text_float / text_len, text_len)

def encode_back(stacked, preact, pooled, audio_unit, audio_len, grad_audio, proj_weight):
    clips = pooled.shape[0]
    steps_count = preact.shape[0] // clips
    radial = lax.optimization_barrier(jnp.sum(audio_unit * grad_audio, axis=-1, keepdims=True))
    grad_embed = ((grad_audio - audio_unit * radial) / audio_len).astype(jnp.bfloat16)
    proj_term = lax.dot_general(pooled, grad_embed, (((0,), (0,)), ((), ())), preferred_element_type=jnp.float32)
    grad_pooled = lax.dot_general(grad_embed, proj_weight, (((1,), (1,)), ((), ())), preferred_element_type=jnp.float32) / steps_count
    grad_act = jnp.broadcast_to(grad_pooled[:, None, :], (clips, steps_count, grad_pooled.shape[1])).reshape(clips * steps_count, -1)
    grad_pre = jax.vjp(jax.nn.gelu, preact)[1](grad_act)[0].astype(jnp.bfloat16)
    conv_term = lax.dot_general(stacked, grad_pre, (((0,), (0,)), ((), ())), preferred_element_type=jnp.float32)
    return (conv_term, proj_term)

def reference(audio_frames, conv_weight, proj_weight, text_embed, pair_langs, log_scale, lang_bias, log_var):
    classes = jnp.arange(LANGS, dtype=jnp.int32)
    onehot_all = (pair_langs.reshape(-1)[:, None] == classes[None, :]).astype(jnp.float32)
    counts = lax.optimization_barrier(jnp.sum(onehot_all, axis=0))
    weight_table = jnp.exp(-log_var) / jnp.maximum(counts, 1.0)
    scale_table = jnp.exp(log_scale)

    def one_group(carry, group_data):
        conv_sum, proj_sum, loss_sum, scale_sum = carry
        frames, text_rows, pair_ids = group_data
        stacked, preact, pooled, audio_unit, audio_len = encode(frames, conv_weight, proj_weight)
        audio_bf = audio_unit.astype(jnp.bfloat16)
        text_unit, text_len = normalize_text(text_rows)
        text_bf = text_unit.astype(jnp.bfloat16)
        onehot = (pair_ids[:, None] == classes[None, :]).astype(jnp.float32)
        pair_scale = lax.optimization_barrier(jnp.sum(onehot * scale_table[None, :], axis=1))
        pair_bias = lax.optimization_barrier(jnp.sum(onehot * lang_bias[None, :], axis=1))
        own_weight = lax.optimization_barrier(jnp.sum(onehot * weight_table[None, :], axis=1))
        logits = pair_scale[:, None] * lax.dot_general(audio_bf, text_bf, (((1,), (1,)), ((), ())), preferred_element_type=jnp.float32) + pair_bias[:, None]
        row_max = lax.optimization_barrier(jnp.max(logits, axis=1))
        row_lse = row_max + jnp.log(lax.optimization_barrier(jnp.sum(jnp.exp(logits - row_max[:, None]), axis=1)))
        col_max = lax.optimization_barrier(jnp.max(logits, axis=0))
        col_lse = col_max + jnp.log(lax.optimization_barrier(jnp.sum(jnp.exp(logits - col_max[None, :]), axis=0)))
        positive = jnp.diagonal(logits)
        pair_loss = 0.5 * (row_lse + col_lse) - positive
        rows_index = jnp.arange(logits.shape[0], dtype=jnp.int32)
        on_diagonal = rows_index[:, None] == rows_index[None, :]
        score_grad = 0.5 * (own_weight[:, None] * jnp.exp(logits - row_lse[:, None]) + own_weight[None, :] * jnp.exp(logits - col_lse[None, :]))
        score_grad = score_grad - jnp.where(on_diagonal, own_weight[:, None], 0.0)
        scale_terms = lax.optimization_barrier(jnp.sum(score_grad * (logits - pair_bias[:, None]), axis=1))
        weighted = (score_grad * pair_scale[:, None]).astype(jnp.bfloat16)
        grad_audio = jnp.dot(weighted, text_bf, preferred_element_type=jnp.float32)
        grad_text = lax.dot_general(weighted, audio_bf, (((0,), (0,)), ((), ())), preferred_element_type=jnp.float32)
        text_grad = (grad_text - text_unit * lax.optimization_barrier(jnp.sum(text_unit * grad_text, axis=1, keepdims=True))) / text_len
        conv_term, proj_term = encode_back(stacked, preact, pooled, audio_unit, audio_len, grad_audio, proj_weight)
        loss_sum = loss_sum + lax.optimization_barrier(jnp.sum(onehot * pair_loss[:, None], axis=0))
        scale_sum = scale_sum + lax.optimization_barrier(jnp.sum(onehot * scale_terms[:, None], axis=0))
        return ((conv_sum + conv_term, proj_sum + proj_term, loss_sum, scale_sum), text_grad)
    start_carry = (jnp.zeros((3 * CIN, WIDTH), jnp.float32), jnp.zeros((WIDTH, EMB), jnp.float32), jnp.zeros((LANGS,), jnp.float32), jnp.zeros((LANGS,), jnp.float32))
    final_carry, text_grad = lax.scan(one_group, start_carry, (audio_frames, text_embed, pair_langs))
    conv_grad, proj_grad, loss_sum, scale_grad = final_carry
    var_weight = jnp.exp(-log_var)
    lang_mean = loss_sum / jnp.maximum(counts, 1.0)
    loss = jnp.sum(var_weight * lang_mean + log_var)
    var_grad = 1.0 - var_weight * lang_mean
    return (loss, scale_grad, var_grad, conv_grad, proj_grad, text_grad)
```

```python
import functools

import jax
import jax.numpy as jnp
from jax import lax
from jax.experimental import pallas as pl
from jax.experimental.pallas import tpu as pltpu
from jax.sharding import PartitionSpec as P

MESH = pl.DeviceIdType.MESH
F32 = jnp.float32
BF16 = jnp.bfloat16
epsilon = 1e-06
LANES = 128
VMEM_BYTES = 58 * 1024 * 1024


def dot(a, b, dims=((1,), (0,))):
    return lax.dot_general(a, b, (dims, ((), ())), preferred_element_type=F32)


def copy_to(src, dst, sends, recvs, index, device):
    return pltpu.make_async_remote_copy(
        src_ref=src,
        dst_ref=dst,
        send_sem=sends.at[index],
        recv_sem=recvs.at[index],
        device_id=device,
        device_id_type=MESH,
    )


def exchange(axis, count, part, sends, recvs):
    me = lax.axis_index(axis)
    return [
        copy_to(part(me), part(me), sends, recvs, o, {axis: lax.rem(me + o, count)})
        for o in range(1, count)
    ]


def greet(n_blk, n_dp):
    barrier = pltpu.get_barrier_semaphore()
    blk, dp = lax.axis_index("blk"), lax.axis_index("dp")
    for o in range(1, n_blk):
        pl.semaphore_signal(
            barrier, inc=1, device_id={"blk": lax.rem(blk + o, n_blk)}, device_id_type=MESH
        )
    for o in range(1, n_dp):
        pl.semaphore_signal(
            barrier, inc=1, device_id={"dp": lax.rem(dp + o, n_dp)}, device_id_type=MESH
        )
    pl.semaphore_wait(barrier, n_blk + n_dp - 2)


def shift_down(values, frame, steps):
    return jnp.where(frame == 0, 0.0, pltpu.roll(values, 1, 0))


def shift_up(values, frame, steps):
    return jnp.where(frame == steps - 1, 0.0, pltpu.roll(values, values.shape[0] - 1, 0))


def step_kernel(
    n_blk, n_dp, steps,
    frames, conv_w, proj_w, text, ids_col, ids_row, tables,
    pre_out, pooled, embed_out, text_term, sums_out,
    all_text, slope, ids_slots, count_slots, stat_slots,
    text_s, text_r, ids_s, ids_r, count_s, count_r, stat_s, stat_r,
):
    rows, cin = frames.shape
    width = conv_w.shape[1]
    clips = rows // steps
    group = ids_row.shape[1]
    blk, dp = lax.axis_index("blk"), lax.axis_index("dp")
    own = pl.ds(pl.multiple_of(blk * clips, clips), clips)

    ids_slots[blk] = ids_row[...]
    text_float = text[...].astype(F32)
    text_len = jnp.sqrt(jnp.sum(text_float * text_float, axis=1, keepdims=True) + epsilon)
    all_text[own, :] = (text_float / text_len).astype(BF16)
    greet(n_blk, n_dp)
    ids_copies = exchange("blk", n_blk, lambda b: ids_slots.at[b], ids_s, ids_r)
    text_copies = exchange(
        "blk", n_blk,
        lambda b: all_text.at[pl.ds(pl.multiple_of(b * clips, clips), clips), :],
        text_s, text_r,
    )
    for copy in ids_copies + text_copies:
        copy.start()

    tile = 256
    frame = lax.broadcasted_iota(jnp.int32, (rows, tile), 0) % steps
    c0, c1 = 0.7978845608028654, 0.044715

    @pl.loop(0, width // tile)
    def _(t):
        cols = pl.ds(pl.multiple_of(t * tile, tile), tile)
        x = dot(frames[...], conv_w[pl.ds(cin, cin), cols])
        x = x + shift_down(dot(frames[...], conv_w[pl.ds(0, cin), cols]), frame, steps)
        x = x + shift_up(dot(frames[...], conv_w[pl.ds(2 * cin, cin), cols]), frame, steps)
        square = x * x
        bend = jnp.tanh(c0 * x * (1.0 + c1 * square))
        half = 0.5 * (1.0 + bend)
        slope[:, cols] = half + 0.5 * x * (1.0 - bend * bend) * (c0 * (1.0 + 3.0 * c1 * square))
        act = (x * half).reshape(clips, steps, tile)
        pooled[:, cols] = (jnp.sum(act, axis=1) * (1.0 / steps)).astype(BF16)

    for copy in ids_copies:
        copy.wait()
    all_ids = ids_slots[0]
    for b in range(1, n_blk):
        all_ids = all_ids + ids_slots[b]
    across = (lax.broadcasted_iota(jnp.int32, (LANES, group), 0) == all_ids).astype(F32)
    eye = (
        lax.broadcasted_iota(jnp.int32, (LANES, LANES), 0)
        == lax.broadcasted_iota(jnp.int32, (LANES, LANES), 1)
    )
    batch_counts = jnp.sum(
        jnp.where(eye, jnp.sum(across, axis=1, keepdims=True), 0.0), axis=0, keepdims=True
    )
    count_slots[dp] = batch_counts
    count_copies = exchange("dp", n_dp, lambda d: count_slots.at[d], count_s, count_r)
    for copy in count_copies:
        copy.start()

    embedding = dot(pooled[...], proj_w[...])
    audio_len = jnp.sqrt(jnp.sum(embedding * embedding, axis=1, keepdims=True) + epsilon)
    audio_unit = embedding / audio_len
    audio_bf = audio_unit.astype(BF16)

    onehot = (lax.broadcasted_iota(jnp.int32, (clips, LANES), 1) == ids_col[...]).astype(F32)
    log_scale, bias, log_var = tables[0:1, :], tables[1:2, :], tables[2:3, :]
    pair_scale = jnp.sum(onehot * jnp.exp(log_scale), axis=1, keepdims=True)
    pair_bias = jnp.sum(onehot * bias, axis=1, keepdims=True)

    for copy in text_copies:
        copy.wait()
    logits = pair_scale * dot(audio_bf, all_text[...], ((1,), (1,))) + pair_bias
    local_max = jnp.max(logits, axis=0, keepdims=True)
    stat_slots[blk, 0:1, :] = local_max
    stat_slots[blk, 1:2, :] = jnp.sum(jnp.exp(logits - local_max), axis=0, keepdims=True)
    stat_copies = exchange("blk", n_blk, lambda b: stat_slots.at[b], stat_s, stat_r)
    for copy in stat_copies:
        copy.start()

    for copy in count_copies:
        copy.wait()
    counts = count_slots[0]
    for d in range(1, n_dp):
        counts = counts + count_slots[d]
    weight_row = jnp.exp(-log_var) / jnp.maximum(counts, 1.0)
    weight_col = jnp.sum(jnp.where(eye, weight_row, 0.0), axis=1, keepdims=True)
    own_weight = jnp.sum(onehot * weight_row, axis=1, keepdims=True)
    col_weight = jnp.sum(across * weight_col, axis=0, keepdims=True)
    row_max = jnp.max(logits, axis=1, keepdims=True)
    row_lse = row_max + jnp.log(jnp.sum(jnp.exp(logits - row_max), axis=1, keepdims=True))
    diagonal = (
        lax.broadcasted_iota(jnp.int32, (clips, group), 1)
        == lax.broadcasted_iota(jnp.int32, (clips, group), 0) + blk * clips
    )
    row_part = own_weight * jnp.exp(logits - row_lse)

    for copy in stat_copies:
        copy.wait()
    joint_max = stat_slots[0, 0:1, :]
    for b in range(1, n_blk):
        joint_max = jnp.maximum(joint_max, stat_slots[b, 0:1, :])
    joint_sum = jnp.zeros_like(joint_max)
    for b in range(n_blk):
        joint_sum = joint_sum + stat_slots[b, 1:2, :] * jnp.exp(
            stat_slots[b, 0:1, :] - joint_max
        )
    col_lse = joint_max + jnp.log(joint_sum)
    score = 0.5 * (row_part + col_weight * jnp.exp(logits - col_lse))
    score = score - jnp.where(diagonal, own_weight, 0.0)
    weighted = (score * pair_scale).astype(BF16)
    grad_audio = dot(weighted, all_text[...])
    radial = jnp.sum(audio_unit * grad_audio, axis=1, keepdims=True)
    grad_embed = ((grad_audio - audio_unit * radial) / audio_len).astype(BF16)
    embed_out[...] = grad_embed
    grad_pooled = dot(grad_embed, proj_w[...], ((1,), (1,))) * (1.0 / steps)
    text_term[...] = dot(weighted, audio_bf, ((0,), (0,))).astype(BF16)

    positive = jnp.sum(jnp.where(diagonal, logits, 0.0), axis=1, keepdims=True)
    own_col = jnp.sum(jnp.where(diagonal, col_lse, 0.0), axis=1, keepdims=True)
    pair_loss = 0.5 * (row_lse + own_col) - positive
    scale_terms = jnp.sum(score * (logits - pair_bias), axis=1, keepdims=True)
    sums_out[0:1, :] = jnp.sum(onehot * pair_loss, axis=0, keepdims=True)
    sums_out[1:2, :] = jnp.sum(onehot * scale_terms, axis=0, keepdims=True)
    sums_out[2:3, :] = counts

    for t in range(width // tile):
        cols = slice(t * tile, (t + 1) * tile)
        spread = jnp.broadcast_to(grad_pooled[:, None, cols], (clips, steps, tile))
        pre = spread.reshape(rows, tile) * slope[:, cols]
        pre_out[1, :, cols] = pre.astype(BF16)
        pre_out[0, :, cols] = shift_up(pre, frame, steps).astype(BF16)
        pre_out[2, :, cols] = shift_down(pre, frame, steps).astype(BF16)


def whole(count):
    return [pl.BlockSpec(memory_space=pltpu.VMEM)] * count


def forward_step(n_blk, n_dp, frames3, conv_weight, proj_weight, text_rows, pair_ids, tables):
    clips, steps, cin = frames3.shape
    rows, width, emb = clips * steps, conv_weight.shape[1], proj_weight.shape[1]
    group = clips * n_blk
    blk = lax.axis_index("blk")
    ids_row = jnp.where(
        jnp.arange(group, dtype=jnp.int32) // clips == blk, jnp.tile(pair_ids, n_blk), 0
    )[None, :]
    dma = pltpu.SemaphoreType.DMA
    return pl.pallas_call(
        functools.partial(step_kernel, n_blk, n_dp, steps),
        out_shape=(
            jax.ShapeDtypeStruct((3, rows, width), BF16),
            jax.ShapeDtypeStruct((clips, width), BF16),
            jax.ShapeDtypeStruct((clips, emb), BF16),
            jax.ShapeDtypeStruct((group, emb), BF16),
            jax.ShapeDtypeStruct((3, LANES), F32),
        ),
        in_specs=whole(7),
        out_specs=tuple(whole(5)),
        scratch_shapes=[
            pltpu.VMEM((group, emb), BF16),
            pltpu.VMEM((rows, width), F32),
            pltpu.VMEM((n_blk, 1, group), jnp.int32),
            pltpu.VMEM((n_dp, 1, LANES), F32),
            pltpu.VMEM((n_blk, 2, group), F32),
            dma((n_blk,)), dma((n_blk,)), dma((n_blk,)), dma((n_blk,)),
            dma((n_dp,)), dma((n_dp,)), dma((n_blk,)), dma((n_blk,)),
        ],
        compiler_params=pltpu.CompilerParams(
            collective_id=0, has_side_effects=True, vmem_limit_bytes=VMEM_BYTES
        ),
        cost_estimate=pl.CostEstimate(
            flops=6 * rows * cin * width, bytes_accessed=20 * 2**20, transcendentals=rows * width
        ),
    )(
        frames3.reshape(rows, cin), conv_weight, proj_weight, text_rows,
        pair_ids[:, None], ids_row, tables,
    )


def reduce_plain(frames, pre, pooled, grad_embed, text_term, sums):
    conv_term = jnp.concatenate(
        [dot(frames, pre[tap], ((0,), (0,))).astype(BF16) for tap in range(3)], axis=0
    )
    proj_term = dot(pooled, grad_embed, ((0,), (0,))).astype(BF16)
    grad_text = lax.psum_scatter(text_term, "blk", scatter_dimension=0, tiled=True).astype(F32)
    totals = lax.psum(sums[:2], ("blk", "dp"))

    def scatter(term):
        half = lax.psum_scatter(term, "dp", scatter_dimension=1, tiled=True)
        return lax.psum_scatter(half, "blk", scatter_dimension=0, tiled=True).astype(F32)

    return scatter(conv_term), scatter(proj_term), grad_text, totals


def local(
    n_blk, n_dp,
    audio_frames, conv_weight, proj_weight, text_embed, pair_langs, log_scale, lang_bias, log_var,
):
    langs = log_scale.shape[0]
    frames3, text_rows, pair_ids = audio_frames[0], text_embed[0], pair_langs[0]
    tables = jnp.pad(jnp.stack([log_scale, lang_bias, log_var]), ((0, 0), (0, LANES - langs)))
    pre, pooled, grad_embed, text_term, sums = forward_step(
        n_blk, n_dp, frames3, conv_weight, proj_weight, text_rows, pair_ids, tables
    )
    frames = frames3.reshape(-1, frames3.shape[2])
    reduce = reduce_plain
    conv_grad, proj_grad, grad_text, totals = reduce(
        frames, pre, pooled, grad_embed, text_term, sums
    )
    text_float = text_rows.astype(F32)
    text_len = jnp.sqrt(jnp.sum(text_float * text_float, axis=-1, keepdims=True) + epsilon)
    text_unit = text_float / text_len
    text_grad = (
        grad_text - text_unit * jnp.sum(text_unit * grad_text, axis=1, keepdims=True)
    ) / text_len
    loss_sum, scale_grad = totals[0, :langs], totals[1, :langs]
    counts = sums[2, :langs]
    var_weight = jnp.exp(-log_var)
    lang_mean = loss_sum / jnp.maximum(counts, 1.0)
    loss = jnp.sum(var_weight * lang_mean + log_var)
    var_grad = 1.0 - var_weight * lang_mean
    return (loss, scale_grad, var_grad, conv_grad, proj_grad, text_grad[None])


def solution(mesh):
    return jax.shard_map(
        functools.partial(local, mesh.shape["blk"], mesh.shape["dp"]),
        mesh=mesh,
        in_specs=(
            P("dp", "blk", None, None),
            P(),
            P(),
            P("dp", "blk", None),
            P("dp", "blk"),
            P(),
            P(),
            P(),
        ),
        out_specs=(P(), P(), P(), P("blk", "dp"), P("blk", "dp"), P("dp", "blk", None)),
        check_vma=False,
    )
```

```python
import functools

import jax
import jax.numpy as jnp
from jax import lax
from jax.experimental import pallas as pl
from jax.experimental.pallas import tpu as pltpu
from jax.sharding import PartitionSpec as P

MESH = pl.DeviceIdType.MESH
F32 = jnp.float32
BF16 = jnp.bfloat16
epsilon = 1e-06
LANES = 128
VMEM_BYTES = 58 * 1024 * 1024


def dot(a, b, dims=((1,), (0,))):
    return lax.dot_general(a, b, (dims, ((), ())), preferred_element_type=F32)


def copy_to(src, dst, sends, recvs, index, device):
    return pltpu.make_async_remote_copy(
        src_ref=src,
        dst_ref=dst,
        send_sem=sends.at[index],
        recv_sem=recvs.at[index],
        device_id=device,
        device_id_type=MESH,
    )


def exchange(axis, count, part, sends, recvs):
    me = lax.axis_index(axis)
    return [
        copy_to(part(me), part(me), sends, recvs, o, {axis: lax.rem(me + o, count)})
        for o in range(1, count)
    ]


def greet(n_blk, n_dp):
    barrier = pltpu.get_barrier_semaphore()
    blk, dp = lax.axis_index("blk"), lax.axis_index("dp")
    for o in range(1, n_blk):
        pl.semaphore_signal(
            barrier, inc=1, device_id={"blk": lax.rem(blk + o, n_blk)}, device_id_type=MESH
        )
    for o in range(1, n_dp):
        pl.semaphore_signal(
            barrier, inc=1, device_id={"dp": lax.rem(dp + o, n_dp)}, device_id_type=MESH
        )
    pl.semaphore_wait(barrier, n_blk + n_dp - 2)


def shift_down(values, frame, steps):
    return jnp.where(frame == 0, 0.0, pltpu.roll(values, 1, 0))


def shift_up(values, frame, steps):
    return jnp.where(frame == steps - 1, 0.0, pltpu.roll(values, values.shape[0] - 1, 0))


def step_kernel(
    n_blk, n_dp, steps,
    frames, conv_w, proj_w, text, ids_col, ids_row, tables,
    pre_out, pooled, embed_out, text_term, sums_out,
    all_text, slope, ids_slots, count_slots, stat_slots,
    text_s, text_r, ids_s, ids_r, count_s, count_r, stat_s, stat_r,
):
    rows, cin = frames.shape
    width = conv_w.shape[1]
    clips = rows // steps
    group = ids_row.shape[1]
    blk, dp = lax.axis_index("blk"), lax.axis_index("dp")
    own = pl.ds(pl.multiple_of(blk * clips, clips), clips)

    ids_slots[blk] = ids_row[...]
    text_float = text[...].astype(F32)
    text_len = jnp.sqrt(jnp.sum(text_float * text_float, axis=1, keepdims=True) + epsilon)
    all_text[own, :] = (text_float / text_len).astype(BF16)
    greet(n_blk, n_dp)
    ids_copies = exchange("blk", n_blk, lambda b: ids_slots.at[b], ids_s, ids_r)
    text_copies = exchange(
        "blk", n_blk,
        lambda b: all_text.at[pl.ds(pl.multiple_of(b * clips, clips), clips), :],
        text_s, text_r,
    )
    for copy in ids_copies + text_copies:
        copy.start()

    tile = 256
    frame = lax.broadcasted_iota(jnp.int32, (rows, tile), 0) % steps
    c0, c1 = 0.7978845608028654, 0.044715

    @pl.loop(0, width // tile)
    def _(t):
        cols = pl.ds(pl.multiple_of(t * tile, tile), tile)
        x = dot(frames[...], conv_w[pl.ds(cin, cin), cols])
        x = x + shift_down(dot(frames[...], conv_w[pl.ds(0, cin), cols]), frame, steps)
        x = x + shift_up(dot(frames[...], conv_w[pl.ds(2 * cin, cin), cols]), frame, steps)
        square = x * x
        bend = jnp.tanh(c0 * x * (1.0 + c1 * square))
        half = 0.5 * (1.0 + bend)
        slope[:, cols] = half + 0.5 * x * (1.0 - bend * bend) * (c0 * (1.0 + 3.0 * c1 * square))
        act = (x * half).reshape(clips, steps, tile)
        pooled[:, cols] = (jnp.sum(act, axis=1) * (1.0 / steps)).astype(BF16)

    for copy in ids_copies:
        copy.wait()
    all_ids = ids_slots[0]
    for b in range(1, n_blk):
        all_ids = all_ids + ids_slots[b]
    across = (lax.broadcasted_iota(jnp.int32, (LANES, group), 0) == all_ids).astype(F32)
    eye = (
        lax.broadcasted_iota(jnp.int32, (LANES, LANES), 0)
        == lax.broadcasted_iota(jnp.int32, (LANES, LANES), 1)
    )
    batch_counts = jnp.sum(
        jnp.where(eye, jnp.sum(across, axis=1, keepdims=True), 0.0), axis=0, keepdims=True
    )
    count_slots[dp] = batch_counts
    count_copies = exchange("dp", n_dp, lambda d: count_slots.at[d], count_s, count_r)
    for copy in count_copies:
        copy.start()

    embedding = dot(pooled[...], proj_w[...])
    audio_len = jnp.sqrt(jnp.sum(embedding * embedding, axis=1, keepdims=True) + epsilon)
    audio_unit = embedding / audio_len
    audio_bf = audio_unit.astype(BF16)

    onehot = (lax.broadcasted_iota(jnp.int32, (clips, LANES), 1) == ids_col[...]).astype(F32)
    log_scale, bias, log_var = tables[0:1, :], tables[1:2, :], tables[2:3, :]
    pair_scale = jnp.sum(onehot * jnp.exp(log_scale), axis=1, keepdims=True)
    pair_bias = jnp.sum(onehot * bias, axis=1, keepdims=True)

    for copy in text_copies:
        copy.wait()
    logits = pair_scale * dot(audio_bf, all_text[...], ((1,), (1,))) + pair_bias
    local_max = jnp.max(logits, axis=0, keepdims=True)
    stat_slots[blk, 0:1, :] = local_max
    stat_slots[blk, 1:2, :] = jnp.sum(jnp.exp(logits - local_max), axis=0, keepdims=True)
    stat_copies = exchange("blk", n_blk, lambda b: stat_slots.at[b], stat_s, stat_r)
    for copy in stat_copies:
        copy.start()

    for copy in count_copies:
        copy.wait()
    counts = count_slots[0]
    for d in range(1, n_dp):
        counts = counts + count_slots[d]
    weight_row = jnp.exp(-log_var) / jnp.maximum(counts, 1.0)
    weight_col = jnp.sum(jnp.where(eye, weight_row, 0.0), axis=1, keepdims=True)
    own_weight = jnp.sum(onehot * weight_row, axis=1, keepdims=True)
    col_weight = jnp.sum(across * weight_col, axis=0, keepdims=True)
    row_max = jnp.max(logits, axis=1, keepdims=True)
    row_lse = row_max + jnp.log(jnp.sum(jnp.exp(logits - row_max), axis=1, keepdims=True))
    diagonal = (
        lax.broadcasted_iota(jnp.int32, (clips, group), 1)
        == lax.broadcasted_iota(jnp.int32, (clips, group), 0) + blk * clips
    )
    row_part = own_weight * jnp.exp(logits - row_lse)

    for copy in stat_copies:
        copy.wait()
    joint_max = stat_slots[0, 0:1, :]
    for b in range(1, n_blk):
        joint_max = jnp.maximum(joint_max, stat_slots[b, 0:1, :])
    joint_sum = jnp.zeros_like(joint_max)
    for b in range(n_blk):
        joint_sum = joint_sum + stat_slots[b, 1:2, :] * jnp.exp(
            stat_slots[b, 0:1, :] - joint_max
        )
    col_lse = joint_max + jnp.log(joint_sum)
    score = 0.5 * (row_part + col_weight * jnp.exp(logits - col_lse))
    score = score - jnp.where(diagonal, own_weight, 0.0)
    weighted = (score * pair_scale).astype(BF16)
    grad_audio = dot(weighted, all_text[...])
    radial = jnp.sum(audio_unit * grad_audio, axis=1, keepdims=True)
    grad_embed = ((grad_audio - audio_unit * radial) / audio_len).astype(BF16)
    embed_out[...] = grad_embed
    grad_pooled = dot(grad_embed, proj_w[...], ((1,), (1,))) * (1.0 / steps)
    text_term[...] = dot(weighted, audio_bf, ((0,), (0,))).astype(BF16)

    positive = jnp.sum(jnp.where(diagonal, logits, 0.0), axis=1, keepdims=True)
    own_col = jnp.sum(jnp.where(diagonal, col_lse, 0.0), axis=1, keepdims=True)
    pair_loss = 0.5 * (row_lse + own_col) - positive
    scale_terms = jnp.sum(score * (logits - pair_bias), axis=1, keepdims=True)
    sums_out[0:1, :] = jnp.sum(onehot * pair_loss, axis=0, keepdims=True)
    sums_out[1:2, :] = jnp.sum(onehot * scale_terms, axis=0, keepdims=True)
    sums_out[2:3, :] = counts

    for t in range(width // tile):
        cols = slice(t * tile, (t + 1) * tile)
        spread = jnp.broadcast_to(grad_pooled[:, None, cols], (clips, steps, tile))
        pre = spread.reshape(rows, tile) * slope[:, cols]
        pre_out[1, :, cols] = pre.astype(BF16)
        pre_out[0, :, cols] = shift_up(pre, frame, steps).astype(BF16)
        pre_out[2, :, cols] = shift_down(pre, frame, steps).astype(BF16)


def whole(count):
    return [pl.BlockSpec(memory_space=pltpu.VMEM)] * count


def forward_step(n_blk, n_dp, frames3, conv_weight, proj_weight, text_rows, pair_ids, tables):
    clips, steps, cin = frames3.shape
    rows, width, emb = clips * steps, conv_weight.shape[1], proj_weight.shape[1]
    group = clips * n_blk
    blk = lax.axis_index("blk")
    ids_row = jnp.where(
        jnp.arange(group, dtype=jnp.int32) // clips == blk, jnp.tile(pair_ids, n_blk), 0
    )[None, :]
    dma = pltpu.SemaphoreType.DMA
    return pl.pallas_call(
        functools.partial(step_kernel, n_blk, n_dp, steps),
        out_shape=(
            jax.ShapeDtypeStruct((3, rows, width), BF16),
            jax.ShapeDtypeStruct((clips, width), BF16),
            jax.ShapeDtypeStruct((clips, emb), BF16),
            jax.ShapeDtypeStruct((group, emb), BF16),
            jax.ShapeDtypeStruct((3, LANES), F32),
        ),
        in_specs=whole(7),
        out_specs=tuple(whole(5)),
        scratch_shapes=[
            pltpu.VMEM((group, emb), BF16),
            pltpu.VMEM((rows, width), F32),
            pltpu.VMEM((n_blk, 1, group), jnp.int32),
            pltpu.VMEM((n_dp, 1, LANES), F32),
            pltpu.VMEM((n_blk, 2, group), F32),
            dma((n_blk,)), dma((n_blk,)), dma((n_blk,)), dma((n_blk,)),
            dma((n_dp,)), dma((n_dp,)), dma((n_blk,)), dma((n_blk,)),
        ],
        compiler_params=pltpu.CompilerParams(
            collective_id=0, has_side_effects=True, vmem_limit_bytes=VMEM_BYTES
        ),
        cost_estimate=pl.CostEstimate(
            flops=6 * rows * cin * width, bytes_accessed=20 * 2**20, transcendentals=rows * width
        ),
    )(
        frames3.reshape(rows, cin), conv_weight, proj_weight, text_rows,
        pair_ids[:, None], ids_row, tables,
    )


def reduce_kernel(
    steps,
    frames_t, pre, pooled, grad_embed, text_term, sums,
    conv_out, proj_out, text_out, totals_out,
    parts, core_in, first_in, second_in, z_in, text_in, sum_in, total_in,
    core_s, core_r, first_s, first_r, second_s, second_r, z_s, z_r,
    text_s, text_r, sum_s, sum_r, total_s, total_r,
):
    n_z, n_blk, n_dp = steps, text_in.shape[0], total_in.shape[0]
    blk, dp = lax.axis_index("blk"), lax.axis_index("dp")
    z, x, y, core = blk // 2, blk % 2, dp // 2, dp % 2
    clips = text_in.shape[1]
    cin = frames_t.shape[0]
    wide = conv_out.shape[1]
    conv_rows = conv_out.shape[0]
    proj_rows, proj_cols = proj_out.shape
    half = proj_rows // 2
    tile = 256
    tiles = 2 * conv_rows // tile

    text_in[blk] = text_term[pl.ds(pl.multiple_of(blk * clips, clips), clips), :]
    sum_in[blk] = sums[0:2, :]
    greet(n_blk, n_dp)
    small = exchange("blk", n_blk, lambda b: sum_in.at[b], sum_s, sum_r)
    for copy in small:
        copy.start()

    def compute(s):
        target = lax.rem(z + 1 + s, n_z)
        for m in range(tiles):
            block = target * tiles + m
            tap = block // (cin // tile)
            channel = pl.ds(pl.multiple_of(lax.rem(block, cin // tile) * tile, tile), tile)
            for d in range(n_dp):
                cols = slice(d * wide, (d + 1) * wide)
                term = dot(frames_t[channel, :], pre[tap, :, cols]).astype(BF16)
                row = m * tile
                while row < (m + 1) * tile:
                    side = row // conv_rows
                    stop = min((side + 1) * conv_rows, (m + 1) * tile)
                    parts[(s, d % 2) + order(s, d // 2, side)
                          + (slice(row - side * conv_rows, stop - side * conv_rows),)] = (
                        term[row - m * tile : stop - m * tile]
                    )
                    row = stop
        start = pl.multiple_of(target * 2 * proj_rows, 2 * proj_rows)
        proj_term = dot(
            pooled[:, pl.ds(start, 2 * proj_rows)], grad_embed[...], ((0,), (0,))
        ).astype(BF16)
        for d in range(n_dp):
            for side in range(2):
                for part in range(2):
                    top = side * proj_rows + part * half
                    parts[(s, d % 2) + order(s, d // 2, side)
                          + (slice(conv_rows, conv_rows + half),
                             slice(part * proj_cols, (part + 1) * proj_cols))] = (
                        proj_term[top : top + half, d * proj_cols : (d + 1) * proj_cols]
                    )

    def order(s, along_y, along_x):
        return (along_y, along_x) if s % 2 == 0 else (along_x, along_y)

    y_peer = {"dp": dp + 2 - 4 * y}
    x_peer = {"blk": blk + 1 - 2 * x}
    core_peer = {"dp": dp + 1 - 2 * core}
    core_copy, first_copy, second_copy, z_copy = [], [], [], []
    for s in range(n_z):
        first_at, second_at = order(s, y, x)
        first_peer, second_peer = (y_peer, x_peer) if s % 2 == 0 else (x_peer, y_peer)
        core_copy.append(
            copy_to(parts.at[s, 1 - core], core_in.at[s], core_s, core_r, s, core_peer)
        )
        first_copy.append(
            copy_to(
                parts.at[s, core, 1 - first_at], first_in.at[s], first_s, first_r, s, first_peer
            )
        )
        second_copy.append(
            copy_to(
                parts.at[s, core, first_at, 1 - second_at], second_in.at[s],
                second_s, second_r, s, second_peer,
            )
        )
        if s < n_z - 1:
            target = lax.rem(z + 1 + s, n_z)
            z_copy.append(
                copy_to(
                    parts.at[s, core, first_at, second_at], z_in.at[s], z_s, z_r, s,
                    {"blk": target * 2 + x},
                )
            )

    def add(ref, arrived):
        ref[...] = (ref[...].astype(F32) + arrived[...].astype(F32)).astype(BF16)

    text_copies, total_copies = [], []
    for t in range(n_z + 3):
        if t < n_z:
            compute(t)
            core_copy[t].start()
        if 0 <= t - 1 < n_z:
            s = t - 1
            core_copy[s].wait()
            add(parts.at[s, core], core_in.at[s])
            first_copy[s].start()
        if t == 1:
            for o in range(1, n_blk):
                peer = lax.rem(blk + o, n_blk)
                text_copies.append(
                    copy_to(
                        text_term.at[pl.ds(pl.multiple_of(peer * clips, clips), clips), :],
                        text_in.at[blk], text_s, text_r, o, {"blk": peer},
                    )
                )
                text_copies[-1].start()
            for copy in small:
                copy.wait()
            total = sum_in[0]
            for b in range(1, n_blk):
                total = total + sum_in[b]
            total_in[dp] = total
            total_copies = exchange("dp", n_dp, lambda d: total_in.at[d], total_s, total_r)
            for copy in total_copies:
                copy.start()
        if 0 <= t - 2 < n_z:
            s = t - 2
            first_at, _ = order(s, y, x)
            first_copy[s].wait()
            add(parts.at[s, core, first_at], first_in.at[s])
            second_copy[s].start()
        if 0 <= t - 3 < n_z:
            s = t - 3
            first_at, second_at = order(s, y, x)
            second_copy[s].wait()
            if s < n_z - 1:
                add(parts.at[s, core, first_at, second_at], second_in.at[s])
                z_copy[s].start()

    for copy in total_copies:
        copy.wait()
    total = total_in[0]
    for d in range(1, n_dp):
        total = total + total_in[d]
    totals_out[...] = total
    for copy in text_copies:
        copy.wait()
    grad_text = text_in[0].astype(F32)
    for b in range(1, n_blk):
        grad_text = grad_text + text_in[b].astype(F32)
    text_out[...] = grad_text
    for copy in z_copy:
        copy.wait()
    last = n_z - 1
    first_at, second_at = order(last, y, x)
    whole_sum = parts[last, core, first_at, second_at].astype(F32)
    whole_sum = whole_sum + second_in[last].astype(F32)
    for s in range(last):
        whole_sum = whole_sum + z_in[s].astype(F32)
    conv_out[...] = whole_sum[:conv_rows]
    proj_out[:half, :] = whole_sum[conv_rows:, :proj_cols]
    proj_out[half:, :] = whole_sum[conv_rows:, proj_cols:]


def reduce_fused(n_blk, n_dp, frames, pre, pooled, grad_embed, text_term, sums):
    rows, cin = frames.shape
    width, (clips, emb) = pre.shape[2], grad_embed.shape
    n_z = n_blk // 2
    conv_rows, wide = 3 * cin // n_blk, width // n_dp
    proj_rows, proj_cols = width // n_blk, emb // n_dp
    height = conv_rows + proj_rows // 2
    dma = pltpu.SemaphoreType.DMA
    return pl.pallas_call(
        functools.partial(reduce_kernel, n_z),
        out_shape=(
            jax.ShapeDtypeStruct((conv_rows, wide), F32),
            jax.ShapeDtypeStruct((proj_rows, proj_cols), F32),
            jax.ShapeDtypeStruct((clips, emb), F32),
            jax.ShapeDtypeStruct((2, LANES), F32),
        ),
        in_specs=whole(6),
        out_specs=tuple(whole(4)),
        scratch_shapes=[
            pltpu.VMEM((n_z, 2, 2, 2, height, wide), BF16),
            pltpu.VMEM((n_z, 2, 2, height, wide), BF16),
            pltpu.VMEM((n_z, 2, height, wide), BF16),
            pltpu.VMEM((n_z, height, wide), BF16),
            pltpu.VMEM((n_z, height, wide), BF16),
            pltpu.VMEM((n_blk, clips, emb), BF16),
            pltpu.VMEM((n_blk, 2, LANES), F32),
            pltpu.VMEM((n_dp, 2, LANES), F32),
        ]
        + [dma((n_z,))] * 8
        + [dma((n_blk,))] * 4
        + [dma((n_dp,))] * 2,
        compiler_params=pltpu.CompilerParams(
            collective_id=1, has_side_effects=True, vmem_limit_bytes=VMEM_BYTES
        ),
        cost_estimate=pl.CostEstimate(
            flops=6 * rows * cin * width, bytes_accessed=10 * 2**20, transcendentals=0
        ),
    )(frames.T, pre, pooled, grad_embed, text_term, sums)


def reduce_plain(frames, pre, pooled, grad_embed, text_term, sums):
    conv_term = jnp.concatenate(
        [dot(frames, pre[tap], ((0,), (0,))).astype(BF16) for tap in range(3)], axis=0
    )
    proj_term = dot(pooled, grad_embed, ((0,), (0,))).astype(BF16)
    grad_text = lax.psum_scatter(text_term, "blk", scatter_dimension=0, tiled=True).astype(F32)
    totals = lax.psum(sums[:2], ("blk", "dp"))

    def scatter(term):
        half = lax.psum_scatter(term, "dp", scatter_dimension=1, tiled=True)
        return lax.psum_scatter(half, "blk", scatter_dimension=0, tiled=True).astype(F32)

    return scatter(conv_term), scatter(proj_term), grad_text, totals


def local(
    n_blk, n_dp,
    audio_frames, conv_weight, proj_weight, text_embed, pair_langs, log_scale, lang_bias, log_var,
):
    langs = log_scale.shape[0]
    frames3, text_rows, pair_ids = audio_frames[0], text_embed[0], pair_langs[0]
    tables = jnp.pad(jnp.stack([log_scale, lang_bias, log_var]), ((0, 0), (0, LANES - langs)))
    pre, pooled, grad_embed, text_term, sums = forward_step(
        n_blk, n_dp, frames3, conv_weight, proj_weight, text_rows, pair_ids, tables
    )
    frames = frames3.reshape(-1, frames3.shape[2])
    boxed = n_dp == 4 and n_blk % 2 == 0 and conv_weight.shape[1] // n_dp == 2 * LANES
    reduce = functools.partial(reduce_fused, n_blk, n_dp) if boxed else reduce_plain
    conv_grad, proj_grad, grad_text, totals = reduce(
        frames, pre, pooled, grad_embed, text_term, sums
    )
    text_float = text_rows.astype(F32)
    text_len = jnp.sqrt(jnp.sum(text_float * text_float, axis=-1, keepdims=True) + epsilon)
    text_unit = text_float / text_len
    text_grad = (
        grad_text - text_unit * jnp.sum(text_unit * grad_text, axis=1, keepdims=True)
    ) / text_len
    loss_sum, scale_grad = totals[0, :langs], totals[1, :langs]
    counts = sums[2, :langs]
    var_weight = jnp.exp(-log_var)
    lang_mean = loss_sum / jnp.maximum(counts, 1.0)
    loss = jnp.sum(var_weight * lang_mean + log_var)
    var_grad = 1.0 - var_weight * lang_mean
    return (loss, scale_grad, var_grad, conv_grad, proj_grad, text_grad[None])


def solution(mesh):
    return jax.shard_map(
        functools.partial(local, mesh.shape["blk"], mesh.shape["dp"]),
        mesh=mesh,
        in_specs=(
            P("dp", "blk", None, None),
            P(),
            P(),
            P("dp", "blk", None),
            P("dp", "blk"),
            P(),
            P(),
            P(),
        ),
        out_specs=(P(), P(), P(), P("blk", "dp"), P("blk", "dp"), P("dp", "blk", None)),
        check_vma=False,
    )
```

```python
import functools

import jax
import jax.numpy as jnp
from jax import lax
from jax.experimental import pallas as pl
from jax.experimental.pallas import tpu as pltpu
from jax.sharding import PartitionSpec as P

MESH = pl.DeviceIdType.MESH
F32 = jnp.float32
BF16 = jnp.bfloat16
epsilon = 1e-06
LANES = 128
VMEM_BYTES = 58 * 1024 * 1024


def dot(a, b, dims=((1,), (0,))):
    return lax.dot_general(a, b, (dims, ((), ())), preferred_element_type=F32)


def copy_to(src, dst, sends, recvs, index, device):
    return pltpu.make_async_remote_copy(
        src_ref=src,
        dst_ref=dst,
        send_sem=sends.at[index],
        recv_sem=recvs.at[index],
        device_id=device,
        device_id_type=MESH,
    )


def exchange(axis, count, part, sends, recvs):
    me = lax.axis_index(axis)
    return [
        copy_to(part(me), part(me), sends, recvs, o, {axis: lax.rem(me + o, count)})
        for o in range(1, count)
    ]


def greet(n_blk, n_dp):
    barrier = pltpu.get_barrier_semaphore()
    blk, dp = lax.axis_index("blk"), lax.axis_index("dp")
    for o in range(1, n_blk):
        pl.semaphore_signal(
            barrier, inc=1, device_id={"blk": lax.rem(blk + o, n_blk)}, device_id_type=MESH
        )
    for o in range(1, n_dp):
        pl.semaphore_signal(
            barrier, inc=1, device_id={"dp": lax.rem(dp + o, n_dp)}, device_id_type=MESH
        )
    pl.semaphore_wait(barrier, n_blk + n_dp - 2)


def shift_down(values, frame, steps):
    return jnp.where(frame == 0, 0.0, pltpu.roll(values, 1, 0))


def shift_up(values, frame, steps):
    return jnp.where(frame == steps - 1, 0.0, pltpu.roll(values, values.shape[0] - 1, 0))


def step_kernel(
    n_blk, n_dp, steps,
    frames, conv_w, proj_w, text, ids, log_scale_in, bias_in, log_var_in,
    pre_out, pooled, embed_out, text_term, sums_out,
    all_text, slope, tables, ids_slots, count_slots, stat_slots,
    text_s, text_r, ids_s, ids_r, count_s, count_r, stat_s, stat_r,
    frames_t=None,
):
    rows, cin = frames.shape
    width = conv_w.shape[1]
    clips = rows // steps
    group = all_text.shape[0]
    langs = log_var_in.shape[1]
    blk, dp = lax.axis_index("blk"), lax.axis_index("dp")
    own = pl.ds(pl.multiple_of(blk * clips, clips), clips)

    tables[...] = jnp.zeros_like(tables)
    tables[0:1, :langs] = log_scale_in[...]
    tables[1:2, :langs] = bias_in[...]
    tables[2:3, :langs] = log_var_in[...]
    diagonal = (
        lax.broadcasted_iota(jnp.int32, (clips, group), 1)
        == lax.broadcasted_iota(jnp.int32, (clips, group), 0) + blk * clips
    )
    same = (
        lax.broadcasted_iota(jnp.int32, (clips, clips), 0)
        == lax.broadcasted_iota(jnp.int32, (clips, clips), 1)
    )
    ids_col = jnp.sum(jnp.where(same, ids[...].astype(F32), 0.0), axis=1, keepdims=True)
    ids_slots[blk] = jnp.sum(jnp.where(diagonal, ids_col, 0.0), axis=0, keepdims=True)
    text_float = text[...].astype(F32)
    text_len = jnp.sqrt(jnp.sum(text_float * text_float, axis=1, keepdims=True) + epsilon)
    all_text[own, :] = (text_float / text_len).astype(BF16)
    greet(n_blk, n_dp)
    ids_copies = exchange("blk", n_blk, lambda b: ids_slots.at[b], ids_s, ids_r)
    text_copies = exchange(
        "blk", n_blk,
        lambda b: all_text.at[pl.ds(pl.multiple_of(b * clips, clips), clips), :],
        text_s, text_r,
    )
    for copy in ids_copies + text_copies:
        copy.start()

    tile = 256
    frame = lax.broadcasted_iota(jnp.int32, (rows, tile), 0) % steps
    c0, c1 = 0.7978845608028654, 0.044715

    @pl.loop(0, width // tile)
    def _(t):
        cols = pl.ds(pl.multiple_of(t * tile, tile), tile)
        x = dot(frames[...], conv_w[pl.ds(cin, cin), cols])
        x = x + shift_down(dot(frames[...], conv_w[pl.ds(0, cin), cols]), frame, steps)
        x = x + shift_up(dot(frames[...], conv_w[pl.ds(2 * cin, cin), cols]), frame, steps)
        square = x * x
        bend = jnp.tanh(c0 * x * (1.0 + c1 * square))
        half = 0.5 * (1.0 + bend)
        slope[:, cols] = half + 0.5 * x * (1.0 - bend * bend) * (c0 * (1.0 + 3.0 * c1 * square))
        act = (x * half).reshape(clips, steps, tile)
        pooled[:, cols] = (jnp.sum(act, axis=1) * (1.0 / steps)).astype(BF16)

    for copy in ids_copies:
        copy.wait()
    all_ids = ids_slots[0]
    for b in range(1, n_blk):
        all_ids = all_ids + ids_slots[b]
    across = (
        lax.broadcasted_iota(jnp.int32, (LANES, group), 0) == all_ids.astype(jnp.int32)
    ).astype(F32)
    eye = (
        lax.broadcasted_iota(jnp.int32, (LANES, LANES), 0)
        == lax.broadcasted_iota(jnp.int32, (LANES, LANES), 1)
    )
    batch_counts = jnp.sum(
        jnp.where(eye, jnp.sum(across, axis=1, keepdims=True), 0.0), axis=0, keepdims=True
    )
    count_slots[dp] = batch_counts
    count_copies = exchange("dp", n_dp, lambda d: count_slots.at[d], count_s, count_r)
    for copy in count_copies:
        copy.start()

    embedding = dot(pooled[...], proj_w[...])
    audio_len = jnp.sqrt(jnp.sum(embedding * embedding, axis=1, keepdims=True) + epsilon)
    audio_unit = embedding / audio_len
    audio_bf = audio_unit.astype(BF16)

    onehot = (
        lax.broadcasted_iota(jnp.int32, (clips, LANES), 1) == ids_col.astype(jnp.int32)
    ).astype(F32)
    log_scale, bias, log_var = tables[0:1, :], tables[1:2, :], tables[2:3, :]
    pair_scale = jnp.sum(onehot * jnp.exp(log_scale), axis=1, keepdims=True)
    pair_bias = jnp.sum(onehot * bias, axis=1, keepdims=True)

    for copy in text_copies:
        copy.wait()
    logits = pair_scale * dot(audio_bf, all_text[...], ((1,), (1,))) + pair_bias
    local_max = jnp.max(logits, axis=0, keepdims=True)
    stat_slots[blk, 0:1, :] = local_max
    stat_slots[blk, 1:2, :] = jnp.sum(jnp.exp(logits - local_max), axis=0, keepdims=True)
    stat_copies = exchange("blk", n_blk, lambda b: stat_slots.at[b], stat_s, stat_r)
    for copy in stat_copies:
        copy.start()

    for copy in count_copies:
        copy.wait()
    counts = count_slots[0]
    for d in range(1, n_dp):
        counts = counts + count_slots[d]
    weight_row = jnp.exp(-log_var) / jnp.maximum(counts, 1.0)
    weight_col = jnp.sum(jnp.where(eye, weight_row, 0.0), axis=1, keepdims=True)
    own_weight = jnp.sum(onehot * weight_row, axis=1, keepdims=True)
    col_weight = jnp.sum(across * weight_col, axis=0, keepdims=True)
    row_max = jnp.max(logits, axis=1, keepdims=True)
    row_lse = row_max + jnp.log(jnp.sum(jnp.exp(logits - row_max), axis=1, keepdims=True))
    row_part = own_weight * jnp.exp(logits - row_lse)

    if frames_t is not None:

        @pl.loop(0, cin // tile)
        def _(t):
            cols = pl.ds(pl.multiple_of(t * tile, tile), tile)
            frames_t[cols, :] = frames[:, cols].T

    for copy in stat_copies:
        copy.wait()
    joint_max = stat_slots[0, 0:1, :]
    for b in range(1, n_blk):
        joint_max = jnp.maximum(joint_max, stat_slots[b, 0:1, :])
    joint_sum = jnp.zeros_like(joint_max)
    for b in range(n_blk):
        joint_sum = joint_sum + stat_slots[b, 1:2, :] * jnp.exp(
            stat_slots[b, 0:1, :] - joint_max
        )
    col_lse = joint_max + jnp.log(joint_sum)
    score = 0.5 * (row_part + col_weight * jnp.exp(logits - col_lse))
    score = score - jnp.where(diagonal, own_weight, 0.0)
    weighted = (score * pair_scale).astype(BF16)
    grad_audio = dot(weighted, all_text[...])
    radial = jnp.sum(audio_unit * grad_audio, axis=1, keepdims=True)
    grad_embed = ((grad_audio - audio_unit * radial) / audio_len).astype(BF16)
    embed_out[...] = grad_embed
    grad_pooled = dot(grad_embed, proj_w[...], ((1,), (1,))) * (1.0 / steps)
    text_term[...] = dot(weighted, audio_bf, ((0,), (0,))).astype(BF16)

    positive = jnp.sum(jnp.where(diagonal, logits, 0.0), axis=1, keepdims=True)
    own_col = jnp.sum(jnp.where(diagonal, col_lse, 0.0), axis=1, keepdims=True)
    pair_loss = 0.5 * (row_lse + own_col) - positive
    scale_terms = jnp.sum(score * (logits - pair_bias), axis=1, keepdims=True)
    sums_out[0:1, :] = jnp.sum(onehot * pair_loss, axis=0, keepdims=True)
    sums_out[1:2, :] = jnp.sum(onehot * scale_terms, axis=0, keepdims=True)
    sums_out[2:3, :] = counts

    for t in range(width // tile):
        cols = slice(t * tile, (t + 1) * tile)
        spread = jnp.broadcast_to(grad_pooled[:, None, cols], (clips, steps, tile))
        pre = spread.reshape(rows, tile) * slope[:, cols]
        pre_out[1, :, cols] = pre.astype(BF16)
        pre_out[0, :, cols] = shift_up(pre, frame, steps).astype(BF16)
        pre_out[2, :, cols] = shift_down(pre, frame, steps).astype(BF16)


def whole(count):
    return [pl.BlockSpec(memory_space=pltpu.VMEM)] * count


def step_shapes(n_blk, clips, steps, width, emb):
    return (
        ((3, clips * steps, width), BF16),
        ((clips, width), BF16),
        ((clips, emb), BF16),
        ((clips * n_blk, emb), BF16),
        ((3, LANES), F32),
    )


def step_scratch(n_blk, n_dp, clips, steps, width, emb):
    group = clips * n_blk
    dma = pltpu.SemaphoreType.DMA
    return [
        pltpu.VMEM((group, emb), BF16),
        pltpu.VMEM((clips * steps, width), F32),
        pltpu.VMEM((8, LANES), F32),
        pltpu.VMEM((n_blk, 1, group), F32),
        pltpu.VMEM((n_dp, 1, LANES), F32),
        pltpu.VMEM((n_blk, 2, group), F32),
        dma((n_blk,)), dma((n_blk,)), dma((n_blk,)), dma((n_blk,)),
        dma((n_dp,)), dma((n_dp,)), dma((n_blk,)), dma((n_blk,)),
    ]


def forward_step(n_blk, n_dp, steps, operands):
    frames, conv_weight, proj_weight, text_rows = operands[:4]
    (rows, cin), clips = frames.shape, text_rows.shape[0]
    width, emb = proj_weight.shape
    return pl.pallas_call(
        functools.partial(step_kernel, n_blk, n_dp, steps),
        out_shape=tuple(
            jax.ShapeDtypeStruct(*shape) for shape in step_shapes(n_blk, clips, steps, width, emb)
        ),
        in_specs=whole(8),
        out_specs=tuple(whole(5)),
        scratch_shapes=step_scratch(n_blk, n_dp, clips, steps, width, emb),
        compiler_params=pltpu.CompilerParams(
            collective_id=0, has_side_effects=True, vmem_limit_bytes=VMEM_BYTES
        ),
        cost_estimate=pl.CostEstimate(
            flops=6 * rows * cin * width, bytes_accessed=20 * 2**20, transcendentals=rows * width
        ),
    )(*operands)


def reduce_kernel(
    n_z,
    frames_t, pre, pooled, grad_embed, text_term, sums, text, tables,
    conv_out, proj_out, text_out, totals_out,
    parts, core_in, first_in, second_in, z_in, text_in, sum_in, total_in,
    core_s, core_r, first_s, first_r, second_s, second_r, z_s, z_r,
    text_s, text_r, sum_s, sum_r, total_s, total_r,
):
    n_blk, n_dp = text_in.shape[0], total_in.shape[0]
    blk, dp = lax.axis_index("blk"), lax.axis_index("dp")
    z, x, y, core = blk // 2, blk % 2, dp // 2, dp % 2
    clips = text_in.shape[1]
    cin = frames_t.shape[0]
    wide = conv_out.shape[1]
    conv_rows = conv_out.shape[0]
    proj_rows, proj_cols = proj_out.shape
    half = proj_rows // 2
    tile = 256
    tiles = 2 * conv_rows // tile

    text_in[blk] = text_term[pl.ds(pl.multiple_of(blk * clips, clips), clips), :]
    sum_in[blk] = sums[0:2, :]
    small = exchange("blk", n_blk, lambda b: sum_in.at[b], sum_s, sum_r)
    for copy in small:
        copy.start()

    def compute(s, which):
        target = lax.rem(z + 1 + s, n_z)
        start = pl.multiple_of(target * 2 * proj_rows, 2 * proj_rows)
        for along_y in range(2):
            d = along_y * 2 + which
            cols = pl.ds(pl.multiple_of(d * wide, wide), wide)
            for m in range(tiles):
                block = target * tiles + m
                tap = block // (cin // tile)
                channel = pl.ds(pl.multiple_of(lax.rem(block, cin // tile) * tile, tile), tile)
                term = dot(frames_t[channel, :], pre[tap, :, cols]).astype(BF16)
                row = m * tile
                while row < (m + 1) * tile:
                    side = row // conv_rows
                    stop = min((side + 1) * conv_rows, (m + 1) * tile)
                    at = (s, which) + order(s, along_y, side)
                    parts[at + (slice(row - side * conv_rows, stop - side * conv_rows),)] = (
                        term[row - m * tile : stop - m * tile]
                    )
                    row = stop
            proj_term = dot(
                pooled[:, pl.ds(start, 2 * proj_rows)],
                grad_embed[:, pl.ds(pl.multiple_of(d * proj_cols, proj_cols), proj_cols)],
                ((0,), (0,)),
            ).astype(BF16)
            for side in range(2):
                for part in range(2):
                    top = side * proj_rows + part * half
                    at = (s, which) + order(s, along_y, side)
                    parts[at + (slice(conv_rows, conv_rows + half),
                                slice(part * proj_cols, (part + 1) * proj_cols))] = (
                        proj_term[top : top + half]
                    )

    def order(s, along_y, along_x):
        return (along_y, along_x) if s % 2 == 0 else (along_x, along_y)

    y_peer = {"dp": dp + 2 - 4 * y}
    x_peer = {"blk": blk + 1 - 2 * x}
    core_peer = {"dp": dp + 1 - 2 * core}
    core_copy, first_copy, second_copy, z_copy = [], [], [], []
    for s in range(n_z):
        first_at, second_at = order(s, y, x)
        first_peer, second_peer = (y_peer, x_peer) if s % 2 == 0 else (x_peer, y_peer)
        core_copy.append(
            copy_to(parts.at[s, 1 - core], core_in.at[s], core_s, core_r, s, core_peer)
        )
        first_copy.append(
            copy_to(
                parts.at[s, core, 1 - first_at], first_in.at[s], first_s, first_r, s, first_peer
            )
        )
        second_copy.append(
            copy_to(
                parts.at[s, core, first_at, 1 - second_at], second_in.at[s],
                second_s, second_r, s, second_peer,
            )
        )
        if s < n_z - 1:
            target = lax.rem(z + 1 + s, n_z)
            z_copy.append(
                copy_to(
                    parts.at[s, core, first_at, second_at], z_in.at[s], z_s, z_r, s,
                    {"blk": target * 2 + x},
                )
            )

    def add(ref, arrived):
        ref[...] = (ref[...].astype(F32) + arrived[...].astype(F32)).astype(BF16)

    text_copies, total_copies = [], []
    for t in range(n_z + 3):
        if t < n_z:
            compute(t, 1 - core)
            core_copy[t].start()
            compute(t, core)
        if 0 <= t - 1 < n_z:
            s = t - 1
            core_copy[s].wait()
            add(parts.at[s, core], core_in.at[s])
            first_copy[s].start()
        if t == 1:
            for o in range(1, n_blk):
                peer = lax.rem(blk + o, n_blk)
                text_copies.append(
                    copy_to(
                        text_term.at[pl.ds(pl.multiple_of(peer * clips, clips), clips), :],
                        text_in.at[blk], text_s, text_r, o, {"blk": peer},
                    )
                )
                text_copies[-1].start()
            for copy in small:
                copy.wait()
            total = sum_in[0]
            for b in range(1, n_blk):
                total = total + sum_in[b]
            total_in[dp] = total
            total_copies = exchange("dp", n_dp, lambda d: total_in.at[d], total_s, total_r)
            for copy in total_copies:
                copy.start()
        if 0 <= t - 2 < n_z:
            s = t - 2
            first_at, _ = order(s, y, x)
            first_copy[s].wait()
            add(parts.at[s, core, first_at], first_in.at[s])
            second_copy[s].start()
        if 0 <= t - 3 < n_z:
            s = t - 3
            first_at, second_at = order(s, y, x)
            second_copy[s].wait()
            if s < n_z - 1:
                add(parts.at[s, core, first_at, second_at], second_in.at[s])
                z_copy[s].start()

    for copy in total_copies:
        copy.wait()
    total = total_in[0]
    for d in range(1, n_dp):
        total = total + total_in[d]
    log_var = tables[2:3, :]
    var_weight = jnp.exp(-log_var)
    lang_mean = total[0:1, :] / jnp.maximum(sums[2:3, :], 1.0)
    loss = jnp.sum(var_weight * lang_mean + log_var, axis=1, keepdims=True)
    totals_out[0:1, :] = jnp.broadcast_to(loss, (1, LANES))
    totals_out[1:2, :] = total[1:2, :]
    totals_out[2:3, :] = 1.0 - var_weight * lang_mean
    for copy in text_copies:
        copy.wait()
    grad_text = text_in[0].astype(F32)
    for b in range(1, n_blk):
        grad_text = grad_text + text_in[b].astype(F32)
    text_float = text[...].astype(F32)
    text_len = jnp.sqrt(jnp.sum(text_float * text_float, axis=1, keepdims=True) + epsilon)
    text_unit = text_float / text_len
    radial = jnp.sum(text_unit * grad_text, axis=1, keepdims=True)
    text_out[...] = (grad_text - text_unit * radial) / text_len
    for copy in z_copy:
        copy.wait()
    last = n_z - 1
    first_at, second_at = order(last, y, x)
    whole_sum = parts[last, core, first_at, second_at].astype(F32)
    whole_sum = whole_sum + second_in[last].astype(F32)
    for s in range(last):
        whole_sum = whole_sum + z_in[s].astype(F32)
    conv_out[...] = whole_sum[:conv_rows]
    proj_out[:half, :] = whole_sum[conv_rows:, :proj_cols]
    proj_out[half:, :] = whole_sum[conv_rows:, proj_cols:]


def fused_kernel(n_blk, n_dp, steps, *refs):
    operands, results, rest = refs[:8], refs[8:12], refs[12:]
    kept, frames_t, rest = rest[:5], rest[5], rest[6:]
    step_part, reduce_part = rest[:14], rest[14:]
    step_kernel(n_blk, n_dp, steps, *operands, *kept, *step_part, frames_t=frames_t)
    reduce_kernel(n_blk // 2, frames_t, *kept, operands[3], step_part[2], *results, *reduce_part)


def fused_step(n_blk, n_dp, steps, operands):
    frames, conv_weight, proj_weight, text_rows = operands[:4]
    (rows, cin), clips = frames.shape, text_rows.shape[0]
    width, emb = proj_weight.shape
    n_z = n_blk // 2
    conv_rows, wide = 3 * cin // n_blk, width // n_dp
    proj_rows, proj_cols = width // n_blk, emb // n_dp
    height = conv_rows + proj_rows // 2
    dma = pltpu.SemaphoreType.DMA
    return pl.pallas_call(
        functools.partial(fused_kernel, n_blk, n_dp, steps),
        out_shape=(
            jax.ShapeDtypeStruct((conv_rows, wide), F32),
            jax.ShapeDtypeStruct((proj_rows, proj_cols), F32),
            jax.ShapeDtypeStruct((clips, emb), F32),
            jax.ShapeDtypeStruct((3, LANES), F32),
        ),
        in_specs=whole(8),
        out_specs=tuple(whole(4)),
        scratch_shapes=[
            pltpu.VMEM(*shape) for shape in step_shapes(n_blk, clips, steps, width, emb)
        ]
        + [pltpu.VMEM((cin, rows), BF16)]
        + step_scratch(n_blk, n_dp, clips, steps, width, emb)
        + [
            pltpu.VMEM((n_z, 2, 2, 2, height, wide), BF16),
            pltpu.VMEM((n_z, 2, 2, height, wide), BF16),
            pltpu.VMEM((n_z, 2, height, wide), BF16),
            pltpu.VMEM((n_z, height, wide), BF16),
            pltpu.VMEM((n_z, height, wide), BF16),
            pltpu.VMEM((n_blk, clips, emb), BF16),
            pltpu.VMEM((n_blk, 2, LANES), F32),
            pltpu.VMEM((n_dp, 2, LANES), F32),
        ]
        + [dma((n_z,))] * 8
        + [dma((n_blk,))] * 4
        + [dma((n_dp,))] * 2,
        compiler_params=pltpu.CompilerParams(
            collective_id=1, has_side_effects=True, vmem_limit_bytes=VMEM_BYTES
        ),
        cost_estimate=pl.CostEstimate(
            flops=12 * rows * cin * width, bytes_accessed=10 * 2**20, transcendentals=rows * width
        ),
    )(*operands)


def reduce_plain(frames, pre, pooled, grad_embed, text_term, sums):
    conv_term = jnp.concatenate(
        [dot(frames, pre[tap], ((0,), (0,))).astype(BF16) for tap in range(3)], axis=0
    )
    proj_term = dot(pooled, grad_embed, ((0,), (0,))).astype(BF16)
    grad_text = lax.psum_scatter(text_term, "blk", scatter_dimension=0, tiled=True).astype(F32)
    totals = lax.psum(sums[:2], ("blk", "dp"))

    def scatter(term):
        half = lax.psum_scatter(term, "dp", scatter_dimension=1, tiled=True)
        return lax.psum_scatter(half, "blk", scatter_dimension=0, tiled=True).astype(F32)

    return scatter(conv_term), scatter(proj_term), grad_text, totals


def local(
    n_blk, n_dp,
    audio_frames, conv_weight, proj_weight, text_embed, pair_langs, log_scale, lang_bias, log_var,
):
    langs = log_scale.shape[0]
    steps, cin = audio_frames.shape[2:]
    frames, text_rows = audio_frames[0].reshape(-1, cin), text_embed[0]
    operands = (
        frames, conv_weight, proj_weight, text_rows, pair_langs,
        log_scale[None], lang_bias[None], log_var[None],
    )
    if n_dp == 4 and n_blk % 2 == 0 and conv_weight.shape[1] // n_dp == 2 * LANES:
        conv_grad, proj_grad, text_grad, rows = fused_step(n_blk, n_dp, steps, operands)
        return (
            rows[0, 0], rows[1, :langs], rows[2, :langs], conv_grad, proj_grad, text_grad[None]
        )
    pre, pooled, grad_embed, text_term, sums = forward_step(n_blk, n_dp, steps, operands)
    conv_grad, proj_grad, grad_text, totals = reduce_plain(
        frames, pre, pooled, grad_embed, text_term, sums
    )
    text_float = text_rows.astype(F32)
    text_len = jnp.sqrt(jnp.sum(text_float * text_float, axis=-1, keepdims=True) + epsilon)
    text_unit = text_float / text_len
    text_grad = (
        grad_text - text_unit * jnp.sum(text_unit * grad_text, axis=1, keepdims=True)
    ) / text_len
    loss_sum, scale_grad = totals[0, :langs], totals[1, :langs]
    counts = sums[2, :langs]
    var_weight = jnp.exp(-log_var)
    lang_mean = loss_sum / jnp.maximum(counts, 1.0)
    loss = jnp.sum(var_weight * lang_mean + log_var)
    var_grad = 1.0 - var_weight * lang_mean
    return (loss, scale_grad, var_grad, conv_grad, proj_grad, text_grad[None])


def solution(mesh):
    return jax.shard_map(
        functools.partial(local, mesh.shape["blk"], mesh.shape["dp"]),
        mesh=mesh,
        in_specs=(
            P("dp", "blk", None, None),
            P(),
            P(),
            P("dp", "blk", None),
            P("dp", "blk"),
            P(),
            P(),
            P(),
        ),
        out_specs=(P(), P(), P(), P("blk", "dp"), P("blk", "dp"), P("dp", "blk", None)),
        check_vma=False,
    )
```

```python
import functools

import jax
import jax.numpy as jnp
from jax import lax
from jax.experimental import pallas as pl
from jax.experimental.pallas import tpu as pltpu
from jax.sharding import PartitionSpec as P

MESH = pl.DeviceIdType.MESH
F32 = jnp.float32
BF16 = jnp.bfloat16
epsilon = 1e-06
LANES = 128
VMEM_BYTES = 58 * 1024 * 1024


def dot(a, b, dims=((1,), (0,))):
    return lax.dot_general(a, b, (dims, ((), ())), preferred_element_type=F32)


def copy_to(src, dst, sends, recvs, index, device):
    return pltpu.make_async_remote_copy(
        src_ref=src,
        dst_ref=dst,
        send_sem=sends.at[index],
        recv_sem=recvs.at[index],
        device_id=device,
        device_id_type=MESH,
    )


def exchange(axis, count, part, sends, recvs):
    me = lax.axis_index(axis)
    return [
        copy_to(part(me), part(me), sends, recvs, o, {axis: lax.rem(me + o, count)})
        for o in range(1, count)
    ]


def greet(n_blk, n_dp):
    barrier = pltpu.get_barrier_semaphore()
    blk, dp = lax.axis_index("blk"), lax.axis_index("dp")
    for o in range(1, n_blk):
        pl.semaphore_signal(
            barrier, inc=1, device_id={"blk": lax.rem(blk + o, n_blk)}, device_id_type=MESH
        )
    for o in range(1, n_dp):
        pl.semaphore_signal(
            barrier, inc=1, device_id={"dp": lax.rem(dp + o, n_dp)}, device_id_type=MESH
        )
    pl.semaphore_wait(barrier, n_blk + n_dp - 2)


def shift_down(values, frame, steps):
    return jnp.where(frame == 0, 0.0, pltpu.roll(values, 1, 0))


def shift_up(values, frame, steps):
    return jnp.where(frame == steps - 1, 0.0, pltpu.roll(values, values.shape[0] - 1, 0))


def step_kernel(
    n_blk, n_dp, steps,
    frames, conv_w, proj_w, text, ids, log_scale_in, bias_in, log_var_in,
    pre_out, pooled, embed_out, text_term, sums_out,
    all_text, slope, tables, ids_slots, count_slots, stat_slots,
    text_s, text_r, ids_s, ids_r, count_s, count_r, stat_s, stat_r,
    frames_t=None,
):
    rows, cin = frames.shape
    width = conv_w.shape[1]
    clips = rows // steps
    group = all_text.shape[0]
    langs = log_var_in.shape[1]
    blk, dp = lax.axis_index("blk"), lax.axis_index("dp")
    own = pl.ds(pl.multiple_of(blk * clips, clips), clips)

    tables[...] = jnp.zeros_like(tables)
    tables[0:1, :langs] = log_scale_in[...]
    tables[1:2, :langs] = bias_in[...]
    tables[2:3, :langs] = log_var_in[...]
    diagonal = (
        lax.broadcasted_iota(jnp.int32, (clips, group), 1)
        == lax.broadcasted_iota(jnp.int32, (clips, group), 0) + blk * clips
    )
    same = (
        lax.broadcasted_iota(jnp.int32, (clips, clips), 0)
        == lax.broadcasted_iota(jnp.int32, (clips, clips), 1)
    )
    ids_col = jnp.sum(jnp.where(same, ids[...].astype(F32), 0.0), axis=1, keepdims=True)
    ids_slots[blk] = jnp.sum(jnp.where(diagonal, ids_col, 0.0), axis=0, keepdims=True)
    text_float = text[...].astype(F32)
    text_len = jnp.sqrt(jnp.sum(text_float * text_float, axis=1, keepdims=True) + epsilon)
    all_text[own, :] = (text_float / text_len).astype(BF16)
    greet(n_blk, n_dp)
    ids_copies = exchange("blk", n_blk, lambda b: ids_slots.at[b], ids_s, ids_r)
    text_copies = exchange(
        "blk", n_blk,
        lambda b: all_text.at[pl.ds(pl.multiple_of(b * clips, clips), clips), :],
        text_s, text_r,
    )
    for copy in ids_copies + text_copies:
        copy.start()

    tile = 256
    frame = lax.broadcasted_iota(jnp.int32, (rows, tile), 0) % steps
    c0, c1 = 0.7978845608028654, 0.044715

    @pl.loop(0, width // tile)
    def _(t):
        cols = pl.ds(pl.multiple_of(t * tile, tile), tile)
        x = dot(frames[...], conv_w[pl.ds(cin, cin), cols])
        x = x + shift_down(dot(frames[...], conv_w[pl.ds(0, cin), cols]), frame, steps)
        x = x + shift_up(dot(frames[...], conv_w[pl.ds(2 * cin, cin), cols]), frame, steps)
        square = x * x
        bend = jnp.tanh(c0 * x * (1.0 + c1 * square))
        half = 0.5 * (1.0 + bend)
        slope[:, cols] = half + 0.5 * x * (1.0 - bend * bend) * (c0 * (1.0 + 3.0 * c1 * square))
        act = (x * half).reshape(clips, steps, tile)
        pooled[:, cols] = (jnp.sum(act, axis=1) * (1.0 / steps)).astype(BF16)

    for copy in ids_copies:
        copy.wait()
    all_ids = ids_slots[0]
    for b in range(1, n_blk):
        all_ids = all_ids + ids_slots[b]
    across = (
        lax.broadcasted_iota(jnp.int32, (LANES, group), 0) == all_ids.astype(jnp.int32)
    ).astype(F32)
    eye = (
        lax.broadcasted_iota(jnp.int32, (LANES, LANES), 0)
        == lax.broadcasted_iota(jnp.int32, (LANES, LANES), 1)
    )
    batch_counts = jnp.sum(
        jnp.where(eye, jnp.sum(across, axis=1, keepdims=True), 0.0), axis=0, keepdims=True
    )
    count_slots[dp] = batch_counts
    count_copies = exchange("dp", n_dp, lambda d: count_slots.at[d], count_s, count_r)
    for copy in count_copies:
        copy.start()

    embedding = dot(pooled[...], proj_w[...])
    audio_len = jnp.sqrt(jnp.sum(embedding * embedding, axis=1, keepdims=True) + epsilon)
    audio_unit = embedding / audio_len
    audio_bf = audio_unit.astype(BF16)

    onehot = (
        lax.broadcasted_iota(jnp.int32, (clips, LANES), 1) == ids_col.astype(jnp.int32)
    ).astype(F32)
    log_scale, bias, log_var = tables[0:1, :], tables[1:2, :], tables[2:3, :]
    pair_scale = jnp.sum(onehot * jnp.exp(log_scale), axis=1, keepdims=True)
    pair_bias = jnp.sum(onehot * bias, axis=1, keepdims=True)

    for copy in text_copies:
        copy.wait()
    logits = pair_scale * dot(audio_bf, all_text[...], ((1,), (1,))) + pair_bias
    local_max = jnp.max(logits, axis=0, keepdims=True)
    stat_slots[blk, 0:1, :] = local_max
    stat_slots[blk, 1:2, :] = jnp.sum(jnp.exp(logits - local_max), axis=0, keepdims=True)
    stat_copies = exchange("blk", n_blk, lambda b: stat_slots.at[b], stat_s, stat_r)
    for copy in stat_copies:
        copy.start()

    for copy in count_copies:
        copy.wait()
    counts = count_slots[0]
    for d in range(1, n_dp):
        counts = counts + count_slots[d]
    weight_row = jnp.exp(-log_var) / jnp.maximum(counts, 1.0)
    weight_col = jnp.sum(jnp.where(eye, weight_row, 0.0), axis=1, keepdims=True)
    own_weight = jnp.sum(onehot * weight_row, axis=1, keepdims=True)
    col_weight = jnp.sum(across * weight_col, axis=0, keepdims=True)
    row_max = jnp.max(logits, axis=1, keepdims=True)
    row_lse = row_max + jnp.log(jnp.sum(jnp.exp(logits - row_max), axis=1, keepdims=True))
    row_part = own_weight * jnp.exp(logits - row_lse)

    if frames_t is not None:

        @pl.loop(0, cin // tile)
        def _(t):
            cols = pl.ds(pl.multiple_of(t * tile, tile), tile)
            frames_t[cols, :] = frames[:, cols].T

    for copy in stat_copies:
        copy.wait()
    joint_max = stat_slots[0, 0:1, :]
    for b in range(1, n_blk):
        joint_max = jnp.maximum(joint_max, stat_slots[b, 0:1, :])
    joint_sum = jnp.zeros_like(joint_max)
    for b in range(n_blk):
        joint_sum = joint_sum + stat_slots[b, 1:2, :] * jnp.exp(
            stat_slots[b, 0:1, :] - joint_max
        )
    col_lse = joint_max + jnp.log(joint_sum)
    score = 0.5 * (row_part + col_weight * jnp.exp(logits - col_lse))
    score = score - jnp.where(diagonal, own_weight, 0.0)
    weighted = (score * pair_scale).astype(BF16)
    grad_audio = dot(weighted, all_text[...])
    radial = jnp.sum(audio_unit * grad_audio, axis=1, keepdims=True)
    grad_embed = ((grad_audio - audio_unit * radial) / audio_len).astype(BF16)
    embed_out[...] = grad_embed
    grad_pooled = dot(grad_embed, proj_w[...], ((1,), (1,))) * (1.0 / steps)
    text_term[...] = dot(weighted, audio_bf, ((0,), (0,))).astype(BF16)

    positive = jnp.sum(jnp.where(diagonal, logits, 0.0), axis=1, keepdims=True)
    own_col = jnp.sum(jnp.where(diagonal, col_lse, 0.0), axis=1, keepdims=True)
    pair_loss = 0.5 * (row_lse + own_col) - positive
    scale_terms = jnp.sum(score * (logits - pair_bias), axis=1, keepdims=True)
    sums_out[0:1, :] = jnp.sum(onehot * pair_loss, axis=0, keepdims=True)
    sums_out[1:2, :] = jnp.sum(onehot * scale_terms, axis=0, keepdims=True)
    sums_out[2:3, :] = counts

    for t in range(width // tile):
        cols = slice(t * tile, (t + 1) * tile)
        spread = jnp.broadcast_to(grad_pooled[:, None, cols], (clips, steps, tile))
        pre = spread.reshape(rows, tile) * slope[:, cols]
        pre_out[1, :, cols] = pre.astype(BF16)
        pre_out[0, :, cols] = shift_up(pre, frame, steps).astype(BF16)
        pre_out[2, :, cols] = shift_down(pre, frame, steps).astype(BF16)


def whole(count):
    return [pl.BlockSpec(memory_space=pltpu.VMEM)] * count


def step_shapes(n_blk, clips, steps, width, emb):
    return (
        ((3, clips * steps, width), BF16),
        ((clips, width), BF16),
        ((clips, emb), BF16),
        ((clips * n_blk, emb), BF16),
        ((3, LANES), F32),
    )


def step_scratch(n_blk, n_dp, clips, steps, width, emb):
    group = clips * n_blk
    dma = pltpu.SemaphoreType.DMA
    return [
        pltpu.VMEM((group, emb), BF16),
        pltpu.VMEM((clips * steps, width), F32),
        pltpu.VMEM((8, LANES), F32),
        pltpu.VMEM((n_blk, 1, group), F32),
        pltpu.VMEM((n_dp, 1, LANES), F32),
        pltpu.VMEM((n_blk, 2, group), F32),
        dma((n_blk,)), dma((n_blk,)), dma((n_blk,)), dma((n_blk,)),
        dma((n_dp,)), dma((n_dp,)), dma((n_blk,)), dma((n_blk,)),
    ]


def forward_step(n_blk, n_dp, steps, operands):
    frames, conv_weight, proj_weight, text_rows = operands[:4]
    (rows, cin), clips = frames.shape, text_rows.shape[0]
    width, emb = proj_weight.shape
    return pl.pallas_call(
        functools.partial(step_kernel, n_blk, n_dp, steps),
        out_shape=tuple(
            jax.ShapeDtypeStruct(*shape) for shape in step_shapes(n_blk, clips, steps, width, emb)
        ),
        in_specs=whole(8),
        out_specs=tuple(whole(5)),
        scratch_shapes=step_scratch(n_blk, n_dp, clips, steps, width, emb),
        compiler_params=pltpu.CompilerParams(
            collective_id=0, has_side_effects=True, vmem_limit_bytes=VMEM_BYTES
        ),
        cost_estimate=pl.CostEstimate(
            flops=6 * rows * cin * width, bytes_accessed=20 * 2**20, transcendentals=rows * width
        ),
    )(*operands)


def reduce_kernel(
    n_z,
    frames_t, pre, pooled, grad_embed, text_term, sums, text, tables,
    conv_out, proj_out, text_out, totals_out,
    parts, core_in, first_in, second_in, z_in, text_in, sum_in, total_in,
    core_s, core_r, first_s, first_r, second_s, second_r, z_s, z_r,
    text_s, text_r, sum_s, sum_r, total_s, total_r,
):
    n_blk, n_dp = text_in.shape[0], total_in.shape[0]
    blk, dp = lax.axis_index("blk"), lax.axis_index("dp")
    z, x, y, core = blk // 2, blk % 2, dp // 2, dp % 2
    clips = text_in.shape[1]
    cin = frames_t.shape[0]
    wide = conv_out.shape[1]
    conv_rows = conv_out.shape[0]
    proj_rows, proj_cols = proj_out.shape
    half = proj_rows // 2
    tile = 256
    tiles = 2 * conv_rows // tile

    text_in[blk] = text_term[pl.ds(pl.multiple_of(blk * clips, clips), clips), :]
    sum_in[blk] = sums[0:2, :]
    small = exchange("blk", n_blk, lambda b: sum_in.at[b], sum_s, sum_r)
    for copy in small:
        copy.start()

    def compute(s, which):
        target = lax.rem(z + 1 + s, n_z)
        start = pl.multiple_of(target * 2 * proj_rows, 2 * proj_rows)
        for along_y in range(2):
            d = along_y * 2 + which
            cols = pl.ds(pl.multiple_of(d * wide, wide), wide)
            for m in range(tiles):
                block = target * tiles + m
                tap = block // (cin // tile)
                channel = pl.ds(pl.multiple_of(lax.rem(block, cin // tile) * tile, tile), tile)
                term = dot(frames_t[channel, :], pre[tap, :, cols]).astype(BF16)
                row = m * tile
                while row < (m + 1) * tile:
                    side = row // conv_rows
                    stop = min((side + 1) * conv_rows, (m + 1) * tile)
                    at = (s, which) + order(s, along_y, side)
                    parts[at + (slice(row - side * conv_rows, stop - side * conv_rows),)] = (
                        term[row - m * tile : stop - m * tile]
                    )
                    row = stop
            proj_term = dot(
                pooled[:, pl.ds(start, 2 * proj_rows)],
                grad_embed[:, pl.ds(pl.multiple_of(d * proj_cols, proj_cols), proj_cols)],
                ((0,), (0,)),
            ).astype(BF16)
            for side in range(2):
                for part in range(2):
                    top = side * proj_rows + part * half
                    at = (s, which) + order(s, along_y, side)
                    parts[at + (slice(conv_rows, conv_rows + half),
                                slice(part * proj_cols, (part + 1) * proj_cols))] = (
                        proj_term[top : top + half]
                    )

    def order(s, along_y, along_x):
        return (along_y, along_x) if s % 2 == 0 else (along_x, along_y)

    y_peer = {"dp": dp + 2 - 4 * y}
    x_peer = {"blk": blk + 1 - 2 * x}
    core_peer = {"dp": dp + 1 - 2 * core}
    core_copy, first_copy, second_copy, z_copy = [], [], [], []
    for s in range(n_z):
        first_at, second_at = order(s, y, x)
        first_peer, second_peer = (y_peer, x_peer) if s % 2 == 0 else (x_peer, y_peer)
        core_copy.append(
            copy_to(parts.at[s, 1 - core], core_in.at[s], core_s, core_r, s, core_peer)
        )
        first_copy.append(
            copy_to(
                parts.at[s, core, 1 - first_at], first_in.at[s], first_s, first_r, s, first_peer
            )
        )
        second_copy.append(
            copy_to(
                parts.at[s, core, first_at, 1 - second_at], second_in.at[s],
                second_s, second_r, s, second_peer,
            )
        )
        if s < n_z - 1:
            target = lax.rem(z + 1 + s, n_z)
            z_copy.append(
                copy_to(
                    parts.at[s, core, first_at, second_at], z_in.at[s], z_s, z_r, s,
                    {"blk": target * 2 + x},
                )
            )

    def add(ref, arrived):
        ref[...] = (ref[...].astype(F32) + arrived[...].astype(F32)).astype(BF16)

    text_copies, total_copies = [], []
    compute(0, 1 - core)
    core_copy[0].start()
    for t in range(n_z + 2):
        if t < n_z:
            compute(t, core)
            if t + 1 < n_z:
                compute(t + 1, 1 - core)
                core_copy[t + 1].start()
            core_copy[t].wait()
            add(parts.at[t, core], core_in.at[t])
            first_copy[t].start()
        if t == 1:
            for o in range(1, n_blk):
                peer = lax.rem(blk + o, n_blk)
                text_copies.append(
                    copy_to(
                        text_term.at[pl.ds(pl.multiple_of(peer * clips, clips), clips), :],
                        text_in.at[blk], text_s, text_r, o, {"blk": peer},
                    )
                )
                text_copies[-1].start()
            for copy in small:
                copy.wait()
            total = sum_in[0]
            for b in range(1, n_blk):
                total = total + sum_in[b]
            total_in[dp] = total
            total_copies = exchange("dp", n_dp, lambda d: total_in.at[d], total_s, total_r)
            for copy in total_copies:
                copy.start()
        if 0 <= t - 1 < n_z:
            s = t - 1
            first_at, _ = order(s, y, x)
            first_copy[s].wait()
            add(parts.at[s, core, first_at], first_in.at[s])
            second_copy[s].start()
        if 0 <= t - 2 < n_z:
            s = t - 2
            first_at, second_at = order(s, y, x)
            second_copy[s].wait()
            if s < n_z - 1:
                add(parts.at[s, core, first_at, second_at], second_in.at[s])
                z_copy[s].start()

    for copy in total_copies:
        copy.wait()
    total = total_in[0]
    for d in range(1, n_dp):
        total = total + total_in[d]
    log_var = tables[2:3, :]
    var_weight = jnp.exp(-log_var)
    lang_mean = total[0:1, :] / jnp.maximum(sums[2:3, :], 1.0)
    loss = jnp.sum(var_weight * lang_mean + log_var, axis=1, keepdims=True)
    totals_out[0:1, :] = jnp.broadcast_to(loss, (1, LANES))
    totals_out[1:2, :] = total[1:2, :]
    totals_out[2:3, :] = 1.0 - var_weight * lang_mean
    for copy in text_copies:
        copy.wait()
    grad_text = text_in[0].astype(F32)
    for b in range(1, n_blk):
        grad_text = grad_text + text_in[b].astype(F32)
    text_float = text[...].astype(F32)
    text_len = jnp.sqrt(jnp.sum(text_float * text_float, axis=1, keepdims=True) + epsilon)
    text_unit = text_float / text_len
    radial = jnp.sum(text_unit * grad_text, axis=1, keepdims=True)
    text_out[...] = (grad_text - text_unit * radial) / text_len
    for copy in z_copy:
        copy.wait()
    last = n_z - 1
    first_at, second_at = order(last, y, x)
    whole_sum = parts[last, core, first_at, second_at].astype(F32)
    whole_sum = whole_sum + second_in[last].astype(F32)
    for s in range(last):
        whole_sum = whole_sum + z_in[s].astype(F32)
    conv_out[...] = whole_sum[:conv_rows]
    proj_out[:half, :] = whole_sum[conv_rows:, :proj_cols]
    proj_out[half:, :] = whole_sum[conv_rows:, proj_cols:]


def fused_kernel(n_blk, n_dp, steps, *refs):
    operands, results, rest = refs[:8], refs[8:12], refs[12:]
    kept, frames_t, rest = rest[:5], rest[5], rest[6:]
    step_part, reduce_part = rest[:14], rest[14:]
    step_kernel(n_blk, n_dp, steps, *operands, *kept, *step_part, frames_t=frames_t)
    reduce_kernel(n_blk // 2, frames_t, *kept, operands[3], step_part[2], *results, *reduce_part)


def fused_step(n_blk, n_dp, steps, operands):
    frames, conv_weight, proj_weight, text_rows = operands[:4]
    (rows, cin), clips = frames.shape, text_rows.shape[0]
    width, emb = proj_weight.shape
    n_z = n_blk // 2
    conv_rows, wide = 3 * cin // n_blk, width // n_dp
    proj_rows, proj_cols = width // n_blk, emb // n_dp
    height = conv_rows + proj_rows // 2
    dma = pltpu.SemaphoreType.DMA
    return pl.pallas_call(
        functools.partial(fused_kernel, n_blk, n_dp, steps),
        out_shape=(
            jax.ShapeDtypeStruct((conv_rows, wide), F32),
            jax.ShapeDtypeStruct((proj_rows, proj_cols), F32),
            jax.ShapeDtypeStruct((clips, emb), F32),
            jax.ShapeDtypeStruct((3, LANES), F32),
        ),
        in_specs=whole(8),
        out_specs=tuple(whole(4)),
        scratch_shapes=[
            pltpu.VMEM(*shape) for shape in step_shapes(n_blk, clips, steps, width, emb)
        ]
        + [pltpu.VMEM((cin, rows), BF16)]
        + step_scratch(n_blk, n_dp, clips, steps, width, emb)
        + [
            pltpu.VMEM((n_z, 2, 2, 2, height, wide), BF16),
            pltpu.VMEM((n_z, 2, 2, height, wide), BF16),
            pltpu.VMEM((n_z, 2, height, wide), BF16),
            pltpu.VMEM((n_z, height, wide), BF16),
            pltpu.VMEM((n_z, height, wide), BF16),
            pltpu.VMEM((n_blk, clips, emb), BF16),
            pltpu.VMEM((n_blk, 2, LANES), F32),
            pltpu.VMEM((n_dp, 2, LANES), F32),
        ]
        + [dma((n_z,))] * 8
        + [dma((n_blk,))] * 4
        + [dma((n_dp,))] * 2,
        compiler_params=pltpu.CompilerParams(
            collective_id=1, has_side_effects=True, vmem_limit_bytes=VMEM_BYTES
        ),
        cost_estimate=pl.CostEstimate(
            flops=12 * rows * cin * width, bytes_accessed=10 * 2**20, transcendentals=rows * width
        ),
    )(*operands)


def reduce_plain(frames, pre, pooled, grad_embed, text_term, sums):
    conv_term = jnp.concatenate(
        [dot(frames, pre[tap], ((0,), (0,))).astype(BF16) for tap in range(3)], axis=0
    )
    proj_term = dot(pooled, grad_embed, ((0,), (0,))).astype(BF16)
    grad_text = lax.psum_scatter(text_term, "blk", scatter_dimension=0, tiled=True).astype(F32)
    totals = lax.psum(sums[:2], ("blk", "dp"))

    def scatter(term):
        half = lax.psum_scatter(term, "dp", scatter_dimension=1, tiled=True)
        return lax.psum_scatter(half, "blk", scatter_dimension=0, tiled=True).astype(F32)

    return scatter(conv_term), scatter(proj_term), grad_text, totals


def local(
    n_blk, n_dp,
    audio_frames, conv_weight, proj_weight, text_embed, pair_langs, log_scale, lang_bias, log_var,
):
    langs = log_scale.shape[0]
    steps, cin = audio_frames.shape[2:]
    frames, text_rows = audio_frames[0].reshape(-1, cin), text_embed[0]
    operands = (
        frames, conv_weight, proj_weight, text_rows, pair_langs,
        log_scale[None], lang_bias[None], log_var[None],
    )
    if n_dp == 4 and n_blk % 2 == 0 and conv_weight.shape[1] // n_dp == 2 * LANES:
        conv_grad, proj_grad, text_grad, rows = fused_step(n_blk, n_dp, steps, operands)
        return (
            rows[0, 0], rows[1, :langs], rows[2, :langs], conv_grad, proj_grad, text_grad[None]
        )
    pre, pooled, grad_embed, text_term, sums = forward_step(n_blk, n_dp, steps, operands)
    conv_grad, proj_grad, grad_text, totals = reduce_plain(
        frames, pre, pooled, grad_embed, text_term, sums
    )
    text_float = text_rows.astype(F32)
    text_len = jnp.sqrt(jnp.sum(text_float * text_float, axis=-1, keepdims=True) + epsilon)
    text_unit = text_float / text_len
    text_grad = (
        grad_text - text_unit * jnp.sum(text_unit * grad_text, axis=1, keepdims=True)
    ) / text_len
    loss_sum, scale_grad = totals[0, :langs], totals[1, :langs]
    counts = sums[2, :langs]
    var_weight = jnp.exp(-log_var)
    lang_mean = loss_sum / jnp.maximum(counts, 1.0)
    loss = jnp.sum(var_weight * lang_mean + log_var)
    var_grad = 1.0 - var_weight * lang_mean
    return (loss, scale_grad, var_grad, conv_grad, proj_grad, text_grad[None])


def solution(mesh):
    return jax.shard_map(
        functools.partial(local, mesh.shape["blk"], mesh.shape["dp"]),
        mesh=mesh,
        in_specs=(
            P("dp", "blk", None, None),
            P(),
            P(),
            P("dp", "blk", None),
            P("dp", "blk"),
            P(),
            P(),
            P(),
        ),
        out_specs=(P(), P(), P(), P("blk", "dp"), P("blk", "dp"), P("dp", "blk", None)),
        check_vma=False,
    )
```
